512 devices in a mesh: state: 8 (over x, core), vocab: 64 (over z, y).
Axes of the slice: x: 4, y: 4, z: 16, core: 2. Of those that a mesh axis runs over, the one named last changes fastest.
Arguments:
- token_ids: int32 [7680], P('vocab'), may hold values from 0 to 65535, as said below
- send_counts: int32 [4096], P('vocab'), may hold values from 0 to 5, as said below
- forward_rows: bfloat16 [7680, 16384], P('vocab', 'state'), may hold values from 0.01 to 32, as said below
- backward_rows: bfloat16 [7680, 16384], P('vocab', 'state'), may hold values from 0.01 to 32, as said below
Outputs:
- emission_counts: bfloat16 [16384, 65536], P('state', 'vocab')
The draws below stay inside these ranges and needn't reach their ends.
Inputs may be any that keep to these rules, and one draw needn't show every extreme that they name: `token_ids`: within each aligned block of 120 positions the ids never fall; at most 5 ids of a block lie in one range of 1024 ids (k * 1024 to (k + 1) * 1024 - 1), and at most 3 distinct ids; in every block some range holds exactly 5 ids with exactly 3 distinct ones, and one range holds exactly 5 in every block. `send_counts`: entry b * 64 + k is the number of ids of block b in range k; each block's entries sum to 120. `forward_rows`: positive. `backward_rows`: positive.
All inputs are finite; a program needn't handle non-finite values.
Results may differ from the reference program's by a relative error of at most 0.0095.
Values may be sent and summed in bfloat16 or wider, within the bound.
A program may use at most 64 MiB of HBM per device.

```python
import jax
import jax.numpy as jnp
from jax import lax

S_DEV = 2048
V_DEV = 1024
P_DEV = 120
CAP = 5
MCAP = 3
STATES = 16384
VOCAB = 65536
POSITIONS = 7680
N_STATE = 8
N_VOCAB = 64


def route_plan(key):
    key = jax.random.fold_in(key, 5)
    keys = jax.random.split(key, 7)
    slots = N_VOCAB * CAP
    owner_of = jnp.arange(slots, dtype=jnp.int32) // CAP
    bias = jax.random.randint(keys[0], (N_VOCAB,), 0, 4)
    noise = jax.random.randint(keys[1], (N_VOCAB, slots), 0, 64)
    forced = jax.random.randint(keys[2], (N_VOCAB,), 0, N_VOCAB)
    shared = jax.random.randint(keys[3], (), 0, N_VOCAB)
    prio = noise + 24 * bias[owner_of][None, :]
    prio = prio + 1000 * (owner_of[None, :] == forced[:, None]).astype(jnp.int32)
    prio = prio + 1000 * (owner_of[None, :] == shared).astype(jnp.int32)
    score = prio * slots + jnp.arange(slots, dtype=jnp.int32)[None, :]
    best, chosen = lax.top_k(score, P_DEV)
    dest = (chosen // CAP).astype(jnp.int32)
    lane = (chosen % CAP).astype(jnp.int32)
    counts = jnp.sum((dest[:, :, None] == jnp.arange(N_VOCAB, dtype=jnp.int32)[None, None, :]).astype(jnp.int32), axis=1)
    hot = jax.random.randint(keys[4], (N_VOCAB,), 0, V_DEV)
    stride = MCAP - 1
    spread = jax.random.randint(keys[6], (N_VOCAB, P_DEV), 0, (V_DEV - MCAP) // stride + 1)
    hot_here = hot[dest]
    other = (hot_here + 1 + lane + stride * spread) % V_DEV
    offset = jnp.where(lane >= stride, hot_here, other)
    tokens = jnp.sort(dest * V_DEV + offset, axis=1)
    return (tokens.reshape(-1).astype(jnp.int32), counts.reshape(-1).astype(jnp.int32))


def draw_token_ids(key, part):
    tokens, counts = route_plan(key)
    return tokens


def draw_send_counts(key, part):
    tokens, counts = route_plan(key)
    return counts


def scaled_field(key, pos_span, group_span, noise_lo, noise_hi):
    keys = jax.random.split(key, 3)
    group = S_DEV // 8
    pos_log = jax.random.uniform(keys[0], (POSITIONS, 1), jnp.float32, -pos_span, pos_span)
    group_log = jax.random.uniform(keys[1], (1, STATES // group), jnp.float32, -group_span, group_span)
    noise_log = jax.random.uniform(keys[2], (POSITIONS, STATES), jnp.float32, noise_lo, noise_hi)
    groups = jnp.repeat(jnp.exp(group_log), group, axis=1)
    return (jnp.exp(pos_log) * groups * jnp.exp(noise_log)).astype(jnp.bfloat16)


def draw_forward_rows(key, part):
    key = jax.random.fold_in(key, 11)
    return scaled_field(key, 0.7, 1.1, -0.7, 0.7)


def draw_backward_rows(key, part):
    key = jax.random.fold_in(key, 12)
    return scaled_field(key, 0.7, 1.1, -0.7, 0.7)


def setup_inputs(seed: int = 0) -> dict:
    key_of = jax.random.split(jax.random.key(seed), 5)
    return {
        "token_ids": draw_token_ids(jax.random.fold_in(key_of[4], 71), 0),
        "send_counts": draw_send_counts(jax.random.fold_in(key_of[4], 71), 0),
        "forward_rows": draw_forward_rows(jax.random.fold_in(key_of[4], 71), 0),
        "backward_rows": draw_backward_rows(jax.random.fold_in(key_of[4], 71), 0),
    }


def reference(token_ids, send_counts, forward_rows, backward_rows):
    weights = (forward_rows.astype(jnp.float32) * backward_rows.astype(jnp.float32)).astype(jnp.bfloat16)
    total = jnp.sum(weights.astype(jnp.float32), axis=1)
    scale = STATES / total
    posterior = (weights.astype(jnp.float32) * scale[:, None]).astype(jnp.bfloat16)
    table = send_counts.reshape(N_VOCAB, N_VOCAB)
    ends = jnp.cumsum(table, axis=1)
    ranks = jnp.arange(P_DEV, dtype=jnp.int32)
    owner = jnp.sum((ranks[None, :, None] >= ends[:, None, :]).astype(jnp.int32), axis=2)
    owner = jnp.minimum(owner, N_VOCAB - 1)
    column = (owner * V_DEV + token_ids.reshape(N_VOCAB, P_DEV) % V_DEV).reshape(-1).astype(jnp.int32)
    places = jnp.arange(POSITIONS, dtype=jnp.int32)
    previous = jnp.concatenate([jnp.full((1,), -1, jnp.int32), column[:-1]])
    starting = jnp.logical_or(places % P_DEV == 0, column != previous)
    run_index = (jnp.cumsum(starting.astype(jnp.int32)) - 1).astype(jnp.int32)
    run_total = run_index[-1] + 1
    run_column = jax.ops.segment_max(column, run_index, num_segments=POSITIONS)
    run_column = jnp.where(places < run_total, run_column, 0).astype(jnp.int32)
    slabs = posterior.reshape(POSITIONS, N_STATE, S_DEV).transpose(1, 0, 2)

    def one_slab(slab):
        merged = jax.ops.segment_sum(slab.astype(jnp.float32), run_index, num_segments=POSITIONS).astype(jnp.bfloat16)
        summed = jax.ops.segment_sum(merged.astype(jnp.float32), run_column, num_segments=VOCAB)
        return summed.T.astype(jnp.bfloat16)

    stacked = lax.map(one_slab, slabs)
    return stacked.reshape(STATES, VOCAB)
```

```python
import functools

import jax
import jax.numpy as jnp
from jax import lax
from jax.experimental import pallas as pl
from jax.experimental.pallas import tpu as pltpu
from jax.sharding import PartitionSpec as P

V_DEV = 1024
LANES = 128
SIDE = 4
MESH = pl.DeviceIdType.MESH
F32 = jnp.float32
BF16 = jnp.bfloat16


def peer(i, z, y, depth):
    q = i // SIDE
    h = (q + 1) // 2
    dz = lax.rem(depth // 2 + h * (1 - 2 * lax.rem(q, 2)) + depth, depth)
    dy = lax.rem(i, SIDE) + q // (depth - 1)
    there = lax.rem(z + dz, depth) * SIDE + lax.rem(y + dy, SIDE)
    return there, dz * SIDE + dy


def route(token_row):
    n = token_row.shape[1]
    ids = token_row.astype(F32)
    up = lax.broadcasted_iota(jnp.int32, (n, n), 0)
    across = lax.broadcasted_iota(jnp.int32, (n, n), 1)
    eye = up == across
    before = up < across

    def turn(row):
        return jnp.sum(jnp.where(eye, row, 0.0), axis=1, keepdims=True)

    ids_col = turn(ids)
    owner = jnp.floor(ids * (1.0 / V_DEV))
    owner_col = jnp.floor(ids_col * (1.0 / V_DEV))
    same_id = jnp.where(ids_col == ids, 1.0, 0.0)
    same_owner = jnp.where(owner_col == owner, 1.0, 0.0)
    earlier = jnp.where(before, 1.0, 0.0)
    alone = jnp.where(jnp.sum(same_id, axis=0, keepdims=True) == 1.0, 1.0, 0.0)
    alone_before = jnp.sum(same_owner * earlier * turn(alone), axis=0, keepdims=True)
    raw = jnp.where(alone_before == 0.0, alone, 0.0)
    repeats = jnp.sum(same_id * earlier, axis=0, keepdims=True)
    leads = jnp.where(repeats == 0.0, 1.0 - raw, 0.0)
    lower = jnp.where(ids_col < ids, 1.0, 0.0)
    rank = jnp.sum(same_owner * lower * turn(leads), axis=0, keepdims=True)
    slot = jnp.where(raw == 1.0, 0.0, 1.0 + rank)
    first = jnp.where(repeats == 0.0, 1.0, 0.0)
    return owner, ids - owner * V_DEV, slot, first


def lay(rows, wide, out, base):
    k, width = rows.shape
    parts = width // LANES
    for i in range(parts):
        wide[pl.ds(i, k, stride=parts), :] = rows[:, i * LANES : (i + 1) * LANES]
    out[:, base : base + parts, :] = wide[...].reshape(k, parts, LANES).astype(BF16)


def exchange(
    owners,
    ranks,
    token_ref,
    forward_ref,
    backward_ref,
    got_raw,
    got_pair,
    got_meta,
    weights,
    wide,
    send_raw,
    send_pair,
    send_meta,
    sums,
    norm_send,
    norm_recv,
    raw_send,
    raw_recv,
    pair_send,
    pair_recv,
    meta_send,
    meta_recv,
    own_sem,
):
    depth = owners // SIDE
    me = lax.axis_index("vocab")
    rank = lax.axis_index("state")
    z, y = me // SIDE, lax.rem(me, SIDE)
    parts = send_raw.shape[1]

    barrier = pltpu.get_barrier_semaphore()

    def greet(i, carry):
        there, _ = peer(i, z, y, depth)
        pl.semaphore_signal(barrier, inc=1, device_id={"vocab": there}, device_id_type=MESH)
        return carry

    lax.fori_loop(0, owners - 1, greet, 0)
    for d in range(1, ranks):
        other = lax.rem(rank + d, ranks)
        pl.semaphore_signal(barrier, inc=1, device_id={"state": other}, device_id_type=MESH)

    weights[...] = (forward_ref[...].astype(F32) * backward_ref[...].astype(F32)).astype(BF16)
    count, width = weights.shape
    partial = lax.dot_general(
        jnp.ones((8, width), BF16), weights[...], (((1,), (1,)), ((), ())), preferred_element_type=F32
    )
    sums[rank] = partial[:1]
    owner, column, slot, first = route(token_ref[...])
    owner_of = lax.broadcasted_iota(jnp.int32, (owners, count), 0).astype(F32)
    mine = owner_of == owner
    picks = [jnp.where(jnp.logical_and(mine, slot == s), 1.0, 0.0) for s in (0.0, 1.0, 2.0)]
    raw = jnp.dot(picks[0].astype(BF16), weights[...], preferred_element_type=F32)
    lay(raw, wide, send_raw, 0)

    pl.semaphore_wait(barrier, owners - 1 + ranks - 1)

    for d in range(1, ranks):
        other = lax.rem(rank + d, ranks)
        pltpu.make_async_remote_copy(
            src_ref=sums.at[rank],
            dst_ref=sums.at[rank],
            send_sem=norm_send,
            recv_sem=norm_recv.at[d - 1],
            device_id={"state": other},
            device_id_type=MESH,
        ).start()

    def push_raw(i, carry):
        there, offset = peer(i, z, y, depth)
        pltpu.make_async_remote_copy(
            src_ref=send_raw.at[there],
            dst_ref=got_raw.at[offset],
            send_sem=raw_send,
            recv_sem=raw_recv,
            device_id={"vocab": there},
            device_id_type=MESH,
        ).start()
        return carry

    lax.fori_loop(0, owners - 1, push_raw, 0)
    own_raw = pltpu.make_async_copy(send_raw.at[me], got_raw.at[0], own_sem.at[0])
    own_raw.start()

    for d in range(1, ranks):
        source = lax.rem(rank + ranks - d, ranks)
        pltpu.make_async_copy(sums.at[source], sums.at[source], norm_recv.at[d - 1]).wait()
    total = sums[0]
    for d in range(1, ranks):
        total = total + sums[d]
    scale = (ranks * width) / total
    eye = lax.broadcasted_iota(jnp.int32, (count, count), 0) == lax.broadcasted_iota(
        jnp.int32, (count, count), 1
    )
    scale_col = jnp.sum(jnp.where(eye, scale, 0.0), axis=1, keepdims=True)
    posterior = (weights[...].astype(F32) * scale_col).astype(BF16)
    for s in (1, 2):
        merged = jnp.dot(picks[s].astype(BF16), posterior, preferred_element_type=F32)
        lay(merged, wide, send_pair, (s - 1) * parts)
    lane = lax.broadcasted_iota(jnp.int32, (owners, LANES), 1)
    meta = jnp.zeros((owners, LANES), F32)
    for s in range(3):
        here = picks[s] * first
        ids = jnp.sum(here * (column + 1.0), axis=1, keepdims=True) - 1.0
        meta = jnp.where(lane == s, ids, meta)
    meta = jnp.where(lane == 3, jnp.sum(picks[0] * scale, axis=1, keepdims=True), meta)
    send_meta[...] = meta.reshape(owners, 1, LANES)

    def push_pair(i, carry):
        there, offset = peer(i, z, y, depth)
        pltpu.make_async_remote_copy(
            src_ref=send_pair.at[there],
            dst_ref=got_pair.at[offset],
            send_sem=pair_send,
            recv_sem=pair_recv,
            device_id={"vocab": there},
            device_id_type=MESH,
        ).start()
        pltpu.make_async_remote_copy(
            src_ref=send_meta.at[there],
            dst_ref=got_meta.at[offset],
            send_sem=meta_send,
            recv_sem=meta_recv,
            device_id={"vocab": there},
            device_id_type=MESH,
        ).start()
        return carry

    lax.fori_loop(0, owners - 1, push_pair, 0)
    own_pair = pltpu.make_async_copy(send_pair.at[me], got_pair.at[0], own_sem.at[1])
    own_pair.start()
    own_meta = pltpu.make_async_copy(send_meta.at[me], got_meta.at[0], own_sem.at[2])
    own_meta.start()

    own_raw.wait()
    own_pair.wait()
    own_meta.wait()
    rest = pl.ds(1, owners - 1)
    for ref, sem in ((got_raw, raw_recv), (got_pair, pair_recv), (got_meta, meta_recv)):
        pltpu.make_async_copy(ref.at[rest], ref.at[rest], sem).wait()
    for ref, sem in ((send_raw, raw_send), (send_pair, pair_send), (send_meta, meta_send)):
        pltpu.make_async_copy(ref.at[rest], ref.at[rest], sem).wait()
    others = pl.ds(1, ranks - 1)
    pltpu.make_async_copy(sums.at[others], sums.at[others], norm_send).wait()


def place(raw_ref, pair_ref, meta_ref, out_ref, wide_raw, wide_pair, onehot, block, sems):
    owners, parts, _ = raw_ref.shape
    wide_raw[...] = raw_ref[...].reshape(owners * parts, LANES).astype(F32)
    wide_pair[...] = pair_ref[...].reshape(owners * 2 * parts, LANES).astype(F32)
    meta = meta_ref[...].reshape(owners, LANES)
    ids = lax.broadcasted_iota(jnp.int32, (owners, V_DEV), 1).astype(F32)
    for s in range(3):
        hit = jnp.where(meta[:, s : s + 1] == ids, 1.0, 0.0)
        onehot[s * owners : (s + 1) * owners, :] = hit.astype(BF16)
    scale = meta[:, 3:4]
    copies = []
    for i in range(parts):
        lone = wide_raw[pl.ds(i, owners, stride=parts), :] * scale
        one = wide_pair[pl.ds(i, owners, stride=2 * parts), :]
        two = wide_pair[pl.ds(parts + i, owners, stride=2 * parts), :]
        rows = jnp.concatenate([lone.astype(BF16), one.astype(BF16), two.astype(BF16)], axis=0)
        counts = lax.dot_general(
            rows, onehot[...], (((0,), (0,)), ((), ())), preferred_element_type=F32
        )
        here = pl.ds(i * LANES, LANES)
        block[here, :] = counts.astype(BF16)
        copy = pltpu.make_async_copy(block.at[here], out_ref.at[here], sems.at[i])
        copy.start()
        copies.append(copy)
    for copy in copies:
        copy.wait()


def shards(token_ids, send_counts, forward_rows, backward_rows):
    owners = lax.axis_size("vocab")
    ranks = lax.axis_size("state")
    count, width = forward_rows.shape
    parts = width // LANES
    vmem = pl.BlockSpec(memory_space=pltpu.VMEM)
    anywhere = pl.BlockSpec(memory_space=pl.ANY)
    dma = pltpu.SemaphoreType.DMA
    got = pl.pallas_call(
        functools.partial(exchange, owners, ranks),
        out_shape=(
            jax.ShapeDtypeStruct((owners, parts, LANES), BF16),
            jax.ShapeDtypeStruct((owners, 2 * parts, LANES), BF16),
            jax.ShapeDtypeStruct((owners, 1, LANES), F32),
        ),
        in_specs=[vmem] * 3,
        out_specs=(anywhere,) * 3,
        scratch_shapes=[
            pltpu.VMEM((count, width), BF16),
            pltpu.VMEM((owners * parts, LANES), F32),
            pltpu.VMEM((owners, parts, LANES), BF16),
            pltpu.VMEM((owners, 2 * parts, LANES), BF16),
            pltpu.VMEM((owners, 1, LANES), F32),
            pltpu.VMEM((ranks, 1, count), F32),
            dma,
            dma((ranks - 1,)),
            dma,
            dma,
            dma,
            dma,
            dma,
            dma,
            dma((3,)),
        ],
        compiler_params=pltpu.CompilerParams(
            collective_id=0, has_side_effects=True, vmem_limit_bytes=32 * 1024 * 1024
        ),
    )(token_ids.reshape(1, count), forward_rows, backward_rows)
    return pl.pallas_call(
        place,
        out_shape=jax.ShapeDtypeStruct((width, V_DEV), BF16),
        in_specs=[vmem] * 3,
        out_specs=anywhere,
        scratch_shapes=[
            pltpu.VMEM((owners * parts, LANES), F32),
            pltpu.VMEM((owners * 2 * parts, LANES), F32),
            pltpu.VMEM((3 * owners, V_DEV), BF16),
            pltpu.VMEM((width, V_DEV), BF16),
            dma((parts,)),
        ],
        compiler_params=pltpu.CompilerParams(vmem_limit_bytes=32 * 1024 * 1024),
    )(*got)


def solution(mesh):
    placed = (P("vocab"), P("vocab"), P("vocab", "state"), P("vocab", "state"))
    return jax.shard_map(
        shards, mesh=mesh, in_specs=placed, out_specs=P("state", "vocab"), check_vma=False
    )
```

```python
import functools

import jax
import jax.numpy as jnp
from jax import lax
from jax.experimental import pallas as pl
from jax.experimental.pallas import tpu as pltpu
from jax.sharding import PartitionSpec as P

V_DEV = 1024
LANES = 128
SIDE = 4
MESH = pl.DeviceIdType.MESH
F32 = jnp.float32
BF16 = jnp.bfloat16


def target(k, z, half, to_late):
    late = z // half
    h = (k + 1) // 2
    turn = h * (1 - 2 * lax.rem(k, 2)) + 2 * half
    if to_late:
        return half + lax.rem(z + turn + late * (half // 2), half)
    ranked = lax.rem(k, 2) * (half // 2) + k // 2
    return (1 - late) * lax.rem(z + turn + half // 2, half) + late * ranked


def route(token_row):
    n = token_row.shape[1]
    ids = token_row.astype(F32)
    up = lax.broadcasted_iota(jnp.int32, (n, n), 0)
    across = lax.broadcasted_iota(jnp.int32, (n, n), 1)
    eye = up == across
    before = up < across

    def turn(row):
        return jnp.sum(jnp.where(eye, row, 0.0), axis=1, keepdims=True)

    ids_col = turn(ids)
    owner = jnp.floor(ids * (1.0 / V_DEV))
    owner_col = jnp.floor(ids_col * (1.0 / V_DEV))
    same_id = jnp.where(ids_col == ids, 1.0, 0.0)
    same_owner = jnp.where(owner_col == owner, 1.0, 0.0)
    earlier = jnp.where(before, 1.0, 0.0)
    alone = jnp.where(jnp.sum(same_id, axis=0, keepdims=True) == 1.0, 1.0, 0.0)
    alone_before = jnp.sum(same_owner * earlier * turn(alone), axis=0, keepdims=True)
    raw = jnp.where(alone_before == 0.0, alone, 0.0)
    repeats = jnp.sum(same_id * earlier, axis=0, keepdims=True)
    leads = jnp.where(repeats == 0.0, 1.0 - raw, 0.0)
    lower = jnp.where(ids_col < ids, 1.0, 0.0)
    rank = jnp.sum(same_owner * lower * turn(leads), axis=0, keepdims=True)
    slot = jnp.where(raw == 1.0, 0.0, 1.0 + rank)
    first = jnp.where(repeats == 0.0, 1.0, 0.0)
    return owner, ids - owner * V_DEV, slot, first


def lay(rows, wide, out, base):
    k, width = rows.shape
    parts = width // LANES
    for i in range(parts):
        wide[pl.ds(i, k, stride=parts), :] = rows[:, i * LANES : (i + 1) * LANES]
    out[:, base : base + parts, :] = wide[...].reshape(k, parts, LANES).astype(BF16)


def exchange(
    owners,
    ranks,
    token_ref,
    forward_ref,
    backward_ref,
    got_raw,
    got_pair,
    got_meta,
    token,
    forward,
    backward,
    weights,
    wide,
    send_raw,
    send_pair,
    send_meta,
    sums,
    norm_send,
    norm_recv,
    raw_send,
    raw_recv,
    pair_send,
    pair_recv,
    meta_send,
    meta_recv,
    own_sem,
    load_sem,
    column_in,
    late_in,
):
    depth = owners // SIDE
    me = lax.axis_index("vocab")
    rank = lax.axis_index("state")
    z, y = me // SIDE, lax.rem(me, SIDE)
    parts = send_raw.shape[1]

    loads = [
        pltpu.make_async_copy(source, here, load_sem.at[i])
        for i, (source, here) in enumerate(
            ((token_ref, token), (forward_ref, forward), (backward_ref, backward))
        )
    ]
    for load in loads:
        load.start()

    half = depth // 2
    late = z // half
    ys = [lax.rem(y + dy, SIDE) for dy in range(SIDE)]

    barrier = pltpu.get_barrier_semaphore()

    def greet(**where):
        pl.semaphore_signal(barrier, inc=1, device_id=where, device_id_type=MESH)

    for dz in range(1, half):
        greet(vocab=(late * half + lax.rem(z + dz, half)) * SIDE + y)

    @pl.when(late == 0)
    def _():
        for k in range(half):
            greet(vocab=(half + k) * SIDE + y)

    for dy in range(1, SIDE):
        greet(vocab=z * SIDE + ys[dy])
    for d in range(1, ranks):
        greet(state=lax.rem(rank + d, ranks))

    loads[0].wait()
    count, width = weights.shape
    owner, column, slot, first = route(token[...])
    owner_of = lax.broadcasted_iota(jnp.int32, (owners, count), 0).astype(F32)
    mine = owner_of == owner
    picks = [jnp.where(jnp.logical_and(mine, slot == s), 1.0, 0.0) for s in (0.0, 1.0, 2.0)]
    loads[1].wait()
    loads[2].wait()
    weights[...] = (forward[...].astype(F32) * backward[...].astype(F32)).astype(BF16)
    raw = jnp.dot(picks[0].astype(BF16), weights[...], preferred_element_type=F32)
    lay(raw, wide, send_raw, 0)

    partial = lax.dot_general(
        jnp.ones((8, width), BF16), weights[...], (((1,), (1,)), ((), ())), preferred_element_type=F32
    )
    sums[rank] = partial[:1]

    def push(sources, k, dys, to_late):
        there_z = target(k, z, half, to_late)
        dz = lax.rem(there_z - z + depth, depth)
        for dy in dys:
            there = there_z * SIDE + ys[dy]
            for source, landing, sent, landed in sources:
                pltpu.make_async_remote_copy(
                    src_ref=source.at[there],
                    dst_ref=landing.at[dz * SIDE + dy],
                    send_sem=sent,
                    recv_sem=landed,
                    device_id={"vocab": there},
                    device_id_type=MESH,
                ).start()

    def push_half(sources, dys, to_late, unroll):
        def step(k, carry):
            push(sources, k, dys, to_late)
            return carry

        if unroll:
            for k in range(half - 1):
                push(sources, k, dys, to_late)
        else:
            lax.fori_loop(0, half - 1, step, 0)
        push(sources, half - 1, [dy for dy in dys if dy], to_late)
        if 0 in dys:

            @pl.when(late != int(to_late))
            def _():
                push(sources, half - 1, [0], to_late)

    raw_ways = ((send_raw, got_raw, raw_send, raw_recv),)
    pair_ways = (
        (send_pair, got_pair, pair_send, pair_recv),
        (send_meta, got_meta, meta_send, meta_recv),
    )

    @pl.when(late == 0)
    def _():
        pl.semaphore_wait(barrier, half - 1 + SIDE - 1 + ranks - 1)

    @pl.when(late != 0)
    def _():
        pl.semaphore_wait(barrier, depth - 1 + SIDE - 1 + ranks - 1)

    for dy in range(1, SIDE):
        pl.semaphore_signal(
            column_in, inc=1, device_id={"vocab": z * SIDE + ys[dy]}, device_id_type=MESH
        )
    push_half(raw_ways, [0], False, True)
    for d in range(1, ranks):
        other = lax.rem(rank + d, ranks)
        pltpu.make_async_remote_copy(
            src_ref=sums.at[rank],
            dst_ref=sums.at[rank],
            send_sem=norm_send,
            recv_sem=norm_recv.at[d - 1],
            device_id={"state": other},
            device_id_type=MESH,
        ).start()
    pl.semaphore_wait(column_in, SIDE - 1)

    @pl.when(late != 0)
    def _():
        pl.semaphore_signal(
            late_in,
            inc=1,
            device_id={"vocab": (depth - 1 - z) * SIDE + y},
            device_id_type=MESH,
        )

    push_half(raw_ways, list(range(1, SIDE)), False, True)

    @pl.when(late != 0)
    def _():
        push_half(raw_ways, list(range(SIDE)), True, False)

    own_raw = pltpu.make_async_copy(send_raw.at[me], got_raw.at[0], own_sem.at[0])
    own_raw.start()

    for d in range(1, ranks):
        source = lax.rem(rank + ranks - d, ranks)
        pltpu.make_async_copy(sums.at[source], sums.at[source], norm_recv.at[d - 1]).wait()
    total = sums[0]
    for d in range(1, ranks):
        total = total + sums[d]
    scale = (ranks * width) / total
    eye = lax.broadcasted_iota(jnp.int32, (count, count), 0) == lax.broadcasted_iota(
        jnp.int32, (count, count), 1
    )
    scale_col = jnp.sum(jnp.where(eye, scale, 0.0), axis=1, keepdims=True)
    posterior = (weights[...].astype(F32) * scale_col).astype(BF16)
    for s in (1, 2):
        merged = jnp.dot(picks[s].astype(BF16), posterior, preferred_element_type=F32)
        lay(merged, wide, send_pair, (s - 1) * parts)
    lane = lax.broadcasted_iota(jnp.int32, (owners, LANES), 1)
    meta = jnp.zeros((owners, LANES), F32)
    for s in range(3):
        here = picks[s] * first
        ids = jnp.sum(here * (column + 1.0), axis=1, keepdims=True) - 1.0
        meta = jnp.where(lane == s, ids, meta)
    meta = jnp.where(lane == 3, jnp.sum(picks[0] * scale, axis=1, keepdims=True), meta)
    send_meta[...] = meta.reshape(owners, 1, LANES)

    push_half(pair_ways, list(range(SIDE)), False, False)

    @pl.when(late == 0)
    def _():
        pl.semaphore_wait(late_in, 1)
        push_half(raw_ways, list(range(SIDE)), True, False)

    push_half(pair_ways, list(range(SIDE)), True, False)
    own_pair = pltpu.make_async_copy(send_pair.at[me], got_pair.at[0], own_sem.at[1])
    own_pair.start()
    own_meta = pltpu.make_async_copy(send_meta.at[me], got_meta.at[0], own_sem.at[2])
    own_meta.start()

    own_raw.wait()
    own_pair.wait()
    own_meta.wait()
    rest = pl.ds(1, owners - 1)
    for ref, sem in ((got_raw, raw_recv), (got_pair, pair_recv), (got_meta, meta_recv)):
        pltpu.make_async_copy(ref.at[rest], ref.at[rest], sem).wait()
    for ref, sem in ((send_raw, raw_send), (send_pair, pair_send), (send_meta, meta_send)):
        pltpu.make_async_copy(ref.at[rest], ref.at[rest], sem).wait()
    others = pl.ds(1, ranks - 1)
    pltpu.make_async_copy(sums.at[others], sums.at[others], norm_send).wait()


def place(raw_ref, pair_ref, meta_ref, out_ref, wide_raw, wide_pair, onehot, block, sems):
    owners, parts, _ = raw_ref.shape
    wide_raw[...] = raw_ref[...].reshape(owners * parts, LANES).astype(F32)
    wide_pair[...] = pair_ref[...].reshape(owners * 2 * parts, LANES).astype(F32)
    meta = meta_ref[...].reshape(owners, LANES)
    ids = lax.broadcasted_iota(jnp.int32, (owners, V_DEV), 1).astype(F32)
    for s in range(3):
        hit = jnp.where(meta[:, s : s + 1] == ids, 1.0, 0.0)
        onehot[s * owners : (s + 1) * owners, :] = hit.astype(BF16)
    scale = meta[:, 3:4]
    copies = []
    for i in range(parts):
        lone = wide_raw[pl.ds(i, owners, stride=parts), :] * scale
        one = wide_pair[pl.ds(i, owners, stride=2 * parts), :]
        two = wide_pair[pl.ds(parts + i, owners, stride=2 * parts), :]
        rows = jnp.concatenate([lone.astype(BF16), one.astype(BF16), two.astype(BF16)], axis=0)
        counts = lax.dot_general(
            rows, onehot[...], (((0,), (0,)), ((), ())), preferred_element_type=F32
        )
        here = pl.ds(i * LANES, LANES)
        block[here, :] = counts.astype(BF16)
        copy = pltpu.make_async_copy(block.at[here], out_ref.at[here], sems.at[i])
        copy.start()
        copies.append(copy)
    for copy in copies:
        copy.wait()


def shards(token_ids, send_counts, forward_rows, backward_rows):
    owners = lax.axis_size("vocab")
    ranks = lax.axis_size("state")
    count, width = forward_rows.shape
    parts = width // LANES
    vmem = pl.BlockSpec(memory_space=pltpu.VMEM)
    anywhere = pl.BlockSpec(memory_space=pl.ANY)
    dma = pltpu.SemaphoreType.DMA
    got = pl.pallas_call(
        functools.partial(exchange, owners, ranks),
        out_shape=(
            jax.ShapeDtypeStruct((owners, parts, LANES), BF16),
            jax.ShapeDtypeStruct((owners, 2 * parts, LANES), BF16),
            jax.ShapeDtypeStruct((owners, 1, LANES), F32),
        ),
        in_specs=[pl.BlockSpec(memory_space=pltpu.HBM)] * 3,
        out_specs=(anywhere,) * 3,
        scratch_shapes=[
            pltpu.VMEM((1, count), jnp.int32),
            pltpu.VMEM((count, width), BF16),
            pltpu.VMEM((count, width), BF16),
            pltpu.VMEM((count, width), BF16),
            pltpu.VMEM((owners * parts, LANES), F32),
            pltpu.VMEM((owners, parts, LANES), BF16),
            pltpu.VMEM((owners, 2 * parts, LANES), BF16),
            pltpu.VMEM((owners, 1, LANES), F32),
            pltpu.VMEM((ranks, 1, count), F32),
            dma,
            dma((ranks - 1,)),
            dma,
            dma,
            dma,
            dma,
            dma,
            dma,
            dma((3,)),
            dma((3,)),
            pltpu.SemaphoreType.REGULAR,
            pltpu.SemaphoreType.REGULAR,
        ],
        compiler_params=pltpu.CompilerParams(
            collective_id=0, has_side_effects=True, vmem_limit_bytes=32 * 1024 * 1024
        ),
    )(
        *(
            pltpu.with_memory_space_constraint(operand, pltpu.HBM)
            for operand in (token_ids.reshape(1, count), forward_rows, backward_rows)
        )
    )
    return pl.pallas_call(
        place,
        out_shape=jax.ShapeDtypeStruct((width, V_DEV), BF16),
        in_specs=[vmem] * 3,
        out_specs=anywhere,
        scratch_shapes=[
            pltpu.VMEM((owners * parts, LANES), F32),
            pltpu.VMEM((owners * 2 * parts, LANES), F32),
            pltpu.VMEM((3 * owners, V_DEV), BF16),
            pltpu.VMEM((width, V_DEV), BF16),
            dma((parts,)),
        ],
        compiler_params=pltpu.CompilerParams(vmem_limit_bytes=32 * 1024 * 1024),
    )(*got)


def solution(mesh):
    placed = (P("vocab"), P("vocab"), P("vocab", "state"), P("vocab", "state"))
    return jax.shard_map(
        shards, mesh=mesh, in_specs=placed, out_specs=P("state", "vocab"), check_vma=False
    )
```

```python
import functools

import jax
import jax.numpy as jnp
from jax import lax
from jax.experimental import pallas as pl
from jax.experimental.pallas import tpu as pltpu
from jax.sharding import PartitionSpec as P

V_DEV = 1024
LANES = 128
SIDE = 4
MESH = pl.DeviceIdType.MESH
F32 = jnp.float32
BF16 = jnp.bfloat16


def hop(k, z, depth):
    half = depth // 2
    late = z // half
    last = k // (depth - 1)
    j = k // 2
    minus = lax.rem(k, 2)
    up = half - j
    down = half - 1 - j
    return lax.rem((1 - minus) * up + minus * (depth - down), depth)


def column_order(k, z, depth):
    return k // 2 + lax.rem(k, 2) * (depth // 2)


def route(token_row):
    n = token_row.shape[1]
    ids = token_row.astype(F32)
    up = lax.broadcasted_iota(jnp.int32, (n, n), 0)
    across = lax.broadcasted_iota(jnp.int32, (n, n), 1)
    eye = up == across
    before = up < across

    def turn(row):
        return jnp.sum(jnp.where(eye, row, 0.0), axis=1, keepdims=True)

    ids_col = turn(ids)
    owner = jnp.floor(ids * (1.0 / V_DEV))
    owner_col = jnp.floor(ids_col * (1.0 / V_DEV))
    same_id = jnp.where(ids_col == ids, 1.0, 0.0)
    same_owner = jnp.where(owner_col == owner, 1.0, 0.0)
    earlier = jnp.where(before, 1.0, 0.0)
    alone = jnp.where(jnp.sum(same_id, axis=0, keepdims=True) == 1.0, 1.0, 0.0)
    alone_before = jnp.sum(same_owner * earlier * turn(alone), axis=0, keepdims=True)
    raw = jnp.where(alone_before == 0.0, alone, 0.0)
    repeats = jnp.sum(same_id * earlier, axis=0, keepdims=True)
    leads = jnp.where(repeats == 0.0, 1.0 - raw, 0.0)
    lower = jnp.where(ids_col < ids, 1.0, 0.0)
    rank = jnp.sum(same_owner * lower * turn(leads), axis=0, keepdims=True)
    slot = jnp.where(raw == 1.0, 0.0, 1.0 + rank)
    first = jnp.where(repeats == 0.0, 1.0, 0.0)
    return owner, ids - owner * V_DEV, slot, first


def lay(rows, wide, out, base):
    k, width = rows.shape
    parts = width // LANES
    for i in range(parts):
        wide[pl.ds(i, k, stride=parts), :] = rows[:, i * LANES : (i + 1) * LANES]
    out[:, base : base + parts, :] = wide[...].reshape(k, parts, LANES).astype(BF16)


def exchange(
    owners,
    ranks,
    token_ref,
    forward_ref,
    backward_ref,
    got_raw,
    got_pair,
    got_meta,
    token,
    forward,
    backward,
    weights,
    wide,
    send_raw,
    send_pair,
    send_meta,
    sums,
    norm_send,
    norm_recv,
    raw_send,
    raw_recv,
    pair_send,
    pair_recv,
    meta_send,
    meta_recv,
    own_sem,
    load_sem,
    column_in,
):
    depth = owners // SIDE
    me = lax.axis_index("vocab")
    rank = lax.axis_index("state")
    z, y = me // SIDE, lax.rem(me, SIDE)
    parts = send_raw.shape[1]

    loads = [
        pltpu.make_async_copy(source, here, load_sem.at[i])
        for i, (source, here) in enumerate(
            ((token_ref, token), (forward_ref, forward), (backward_ref, backward))
        )
    ]
    for load in loads:
        load.start()

    ys = [lax.rem(y + dy, SIDE) for dy in range(SIDE)]

    barrier = pltpu.get_barrier_semaphore()

    def greet(**where):
        pl.semaphore_signal(barrier, inc=1, device_id=where, device_id_type=MESH)

    for dz in range(1, depth):
        greet(vocab=lax.rem(z + dz, depth) * SIDE + y)
    for dy in range(1, SIDE):
        greet(vocab=z * SIDE + ys[dy])
    for d in range(1, ranks):
        greet(state=lax.rem(rank + d, ranks))

    loads[0].wait()
    count, width = weights.shape
    owner, column, slot, first = route(token[...])
    owner_of = lax.broadcasted_iota(jnp.int32, (owners, count), 0).astype(F32)
    mine = owner_of == owner
    picks = [jnp.where(jnp.logical_and(mine, slot == s), 1.0, 0.0) for s in (0.0, 1.0, 2.0)]
    loads[1].wait()
    loads[2].wait()
    weights[...] = (forward[...].astype(F32) * backward[...].astype(F32)).astype(BF16)
    raw = jnp.dot(picks[0].astype(BF16), weights[...], preferred_element_type=F32)
    lay(raw, wide, send_raw, 0)

    partial = lax.dot_general(
        jnp.ones((8, width), BF16), weights[...], (((1,), (1,)), ((), ())), preferred_element_type=F32
    )
    sums[rank] = partial[:1]

    def send(sources, there_z, dz, dy):
        there = there_z * SIDE + ys[dy]
        for source, landing, sent, landed in sources:
            pltpu.make_async_remote_copy(
                src_ref=source.at[there],
                dst_ref=landing.at[dz * SIDE + dy],
                send_sem=sent,
                recv_sem=landed,
                device_id={"vocab": there},
                device_id_type=MESH,
            ).start()

    def push(sources, k, dys):
        dz = hop(k, z, depth)
        there_z = lax.rem(z + dz, depth)
        for dy in dys:
            send(sources, there_z, dz, dy)

    def push_all(sources, dys):
        def step(k, carry):
            push(sources, k, dys)
            return carry

        lax.fori_loop(0, depth - 1, step, 0)
        push(sources, depth - 1, [dy for dy in dys if dy])

    def push_column(sources):
        def step(k, carry):
            there_z = column_order(k, z, depth)
            dz = lax.rem(there_z - z + depth, depth)

            @pl.when(dz != 0)
            def _():
                send(sources, there_z, dz, 0)

            for dy in range(1, SIDE):
                send(sources, there_z, dz, dy)
            return carry

        lax.fori_loop(0, depth, step, 0)

    raw_ways = ((send_raw, got_raw, raw_send, raw_recv),)
    pair_ways = (
        (send_pair, got_pair, pair_send, pair_recv),
        (send_meta, got_meta, meta_send, meta_recv),
    )

    pl.semaphore_wait(barrier, depth - 1 + SIDE - 1 + ranks - 1)

    for dy in range(1, SIDE):
        pl.semaphore_signal(
            column_in, inc=1, device_id={"vocab": z * SIDE + ys[dy]}, device_id_type=MESH
        )
    push_all(raw_ways, [0])
    for d in range(1, ranks):
        other = lax.rem(rank + d, ranks)
        pltpu.make_async_remote_copy(
            src_ref=sums.at[rank],
            dst_ref=sums.at[rank],
            send_sem=norm_send,
            recv_sem=norm_recv.at[d - 1],
            device_id={"state": other},
            device_id_type=MESH,
        ).start()
    pl.semaphore_wait(column_in, SIDE - 1)

    push_all(raw_ways, list(range(1, SIDE)))
    own_raw = pltpu.make_async_copy(send_raw.at[me], got_raw.at[0], own_sem.at[0])
    own_raw.start()

    for d in range(1, ranks):
        source = lax.rem(rank + ranks - d, ranks)
        pltpu.make_async_copy(sums.at[source], sums.at[source], norm_recv.at[d - 1]).wait()
    total = sums[0]
    for d in range(1, ranks):
        total = total + sums[d]
    scale = (ranks * width) / total
    eye = lax.broadcasted_iota(jnp.int32, (count, count), 0) == lax.broadcasted_iota(
        jnp.int32, (count, count), 1
    )
    scale_col = jnp.sum(jnp.where(eye, scale, 0.0), axis=1, keepdims=True)
    posterior = (weights[...].astype(F32) * scale_col).astype(BF16)
    for s in (1, 2):
        merged = jnp.dot(picks[s].astype(BF16), posterior, preferred_element_type=F32)
        lay(merged, wide, send_pair, (s - 1) * parts)
    lane = lax.broadcasted_iota(jnp.int32, (owners, LANES), 1)
    meta = jnp.zeros((owners, LANES), F32)
    for s in range(3):
        here = picks[s] * first
        ids = jnp.sum(here * (column + 1.0), axis=1, keepdims=True) - 1.0
        meta = jnp.where(lane == s, ids, meta)
    meta = jnp.where(lane == 3, jnp.sum(picks[0] * scale, axis=1, keepdims=True), meta)
    send_meta[...] = meta.reshape(owners, 1, LANES)

    push_column(pair_ways)
    own_pair = pltpu.make_async_copy(send_pair.at[me], got_pair.at[0], own_sem.at[1])
    own_pair.start()
    own_meta = pltpu.make_async_copy(send_meta.at[me], got_meta.at[0], own_sem.at[2])
    own_meta.start()

    own_raw.wait()
    own_pair.wait()
    own_meta.wait()
    rest = pl.ds(1, owners - 1)
    for ref, sem in ((got_raw, raw_recv), (got_pair, pair_recv), (got_meta, meta_recv)):
        pltpu.make_async_copy(ref.at[rest], ref.at[rest], sem).wait()
    for ref, sem in ((send_raw, raw_send), (send_pair, pair_send), (send_meta, meta_send)):
        pltpu.make_async_copy(ref.at[rest], ref.at[rest], sem).wait()
    others = pl.ds(1, ranks - 1)
    pltpu.make_async_copy(sums.at[others], sums.at[others], norm_send).wait()


def place(raw_ref, pair_ref, meta_ref, out_ref, wide_raw, wide_pair, onehot, block, sems):
    owners, parts, _ = raw_ref.shape
    odd, odd_pair = parts + 1, 2 * parts + 1
    for k in range(owners):
        wide_raw[k * odd : k * odd + parts, :] = raw_ref[k].astype(F32)
        wide_pair[k * odd_pair : k * odd_pair + 2 * parts, :] = pair_ref[k].astype(F32)
    meta = meta_ref[...].reshape(owners, LANES)
    ids = lax.broadcasted_iota(jnp.int32, (owners, V_DEV), 1).astype(F32)
    for s in range(3):
        hit = jnp.where(meta[:, s : s + 1] == ids, 1.0, 0.0)
        onehot[s * owners : (s + 1) * owners, :] = hit.astype(BF16)
    scale = meta[:, 3:4]
    copies = []
    for i in range(parts):
        lone = wide_raw[pl.ds(i, owners, stride=odd), :] * scale
        one = wide_pair[pl.ds(i, owners, stride=odd_pair), :]
        two = wide_pair[pl.ds(parts + i, owners, stride=odd_pair), :]
        rows = jnp.concatenate([lone.astype(BF16), one.astype(BF16), two.astype(BF16)], axis=0)
        counts = lax.dot_general(
            rows, onehot[...], (((0,), (0,)), ((), ())), preferred_element_type=F32
        )
        here = pl.ds(i * LANES, LANES)
        block[here, :] = counts.astype(BF16)
        copy = pltpu.make_async_copy(block.at[here], out_ref.at[here], sems.at[i])
        copy.start()
        copies.append(copy)
    for copy in copies:
        copy.wait()


def shards(token_ids, send_counts, forward_rows, backward_rows):
    owners = lax.axis_size("vocab")
    ranks = lax.axis_size("state")
    count, width = forward_rows.shape
    parts = width // LANES
    vmem = pl.BlockSpec(memory_space=pltpu.VMEM)
    anywhere = pl.BlockSpec(memory_space=pl.ANY)
    dma = pltpu.SemaphoreType.DMA
    got = pl.pallas_call(
        functools.partial(exchange, owners, ranks),
        out_shape=(
            jax.ShapeDtypeStruct((owners, parts, LANES), BF16),
            jax.ShapeDtypeStruct((owners, 2 * parts, LANES), BF16),
            jax.ShapeDtypeStruct((owners, 1, LANES), F32),
        ),
        in_specs=[pl.BlockSpec(memory_space=pltpu.HBM)] * 3,
        out_specs=(anywhere,) * 3,
        scratch_shapes=[
            pltpu.VMEM((1, count), jnp.int32),
            pltpu.VMEM((count, width), BF16),
            pltpu.VMEM((count, width), BF16),
            pltpu.VMEM((count, width), BF16),
            pltpu.VMEM((owners * parts, LANES), F32),
            pltpu.VMEM((owners, parts, LANES), BF16),
            pltpu.VMEM((owners, 2 * parts, LANES), BF16),
            pltpu.VMEM((owners, 1, LANES), F32),
            pltpu.VMEM((ranks, 1, count), F32),
            dma,
            dma((ranks - 1,)),
            dma,
            dma,
            dma,
            dma,
            dma,
            dma,
            dma((3,)),
            dma((3,)),
            pltpu.SemaphoreType.REGULAR,
        ],
        compiler_params=pltpu.CompilerParams(
            collective_id=0, has_side_effects=True, vmem_limit_bytes=32 * 1024 * 1024
        ),
    )(
        *(
            pltpu.with_memory_space_constraint(operand, pltpu.HBM)
            for operand in (token_ids.reshape(1, count), forward_rows, backward_rows)
        )
    )
    return pl.pallas_call(
        place,
        out_shape=jax.ShapeDtypeStruct((width, V_DEV), BF16),
        in_specs=[vmem] * 3,
        out_specs=anywhere,
        scratch_shapes=[
            pltpu.VMEM((owners * (parts + 1), LANES), F32),
            pltpu.VMEM((owners * (2 * parts + 1), LANES), F32),
            pltpu.VMEM((3 * owners, V_DEV), BF16),
            pltpu.VMEM((width, V_DEV), BF16),
            dma((parts,)),
        ],
        compiler_params=pltpu.CompilerParams(vmem_limit_bytes=32 * 1024 * 1024),
    )(*got)


def solution(mesh):
    placed = (P("vocab"), P("vocab"), P("vocab", "state"), P("vocab", "state"))
    return jax.shard_map(
        shards, mesh=mesh, in_specs=placed, out_specs=P("state", "vocab"), check_vma=False
    )
```

```python
import functools

import jax
import jax.numpy as jnp
from jax import lax
from jax.experimental import pallas as pl
from jax.experimental.pallas import tpu as pltpu
from jax.sharding import PartitionSpec as P

V_DEV = 1024
LANES = 128
SIDE = 4
MESH = pl.DeviceIdType.MESH
F32 = jnp.float32
BF16 = jnp.bfloat16


def hop(k, z, depth):
    half = depth // 2
    late = z // half
    last = k // (depth - 1)
    j = k // 2
    minus = lax.rem(k, 2)
    up = half - j
    down = half - 1 - j
    return lax.rem((1 - minus) * up + minus * (depth - down), depth)


def column_order(k, depth):
    return k // 2 + lax.rem(k, 2) * (depth // 2)


def route(token_row):
    n = token_row.shape[1]
    ids = token_row.astype(F32)
    up = lax.broadcasted_iota(jnp.int32, (n, n), 0)
    across = lax.broadcasted_iota(jnp.int32, (n, n), 1)
    eye = up == across
    before = up < across

    def turn(row):
        return jnp.sum(jnp.where(eye, row, 0.0), axis=1, keepdims=True)

    ids_col = turn(ids)
    owner = jnp.floor(ids * (1.0 / V_DEV))
    owner_col = jnp.floor(ids_col * (1.0 / V_DEV))
    same_id = jnp.where(ids_col == ids, 1.0, 0.0)
    same_owner = jnp.where(owner_col == owner, 1.0, 0.0)
    earlier = jnp.where(before, 1.0, 0.0)
    alone = jnp.where(jnp.sum(same_id, axis=0, keepdims=True) == 1.0, 1.0, 0.0)
    alone_before = jnp.sum(same_owner * earlier * turn(alone), axis=0, keepdims=True)
    raw = jnp.where(alone_before == 0.0, alone, 0.0)
    repeats = jnp.sum(same_id * earlier, axis=0, keepdims=True)
    leads = jnp.where(repeats == 0.0, 1.0 - raw, 0.0)
    lower = jnp.where(ids_col < ids, 1.0, 0.0)
    rank = jnp.sum(same_owner * lower * turn(leads), axis=0, keepdims=True)
    slot = jnp.where(raw == 1.0, 0.0, 1.0 + rank)
    first = jnp.where(repeats == 0.0, 1.0, 0.0)
    return owner, ids - owner * V_DEV, slot, first


def lay(rows, wide, out, base):
    k, width = rows.shape
    parts = width // LANES
    for i in range(parts):
        wide[pl.ds(i, k, stride=parts), :] = rows[:, i * LANES : (i + 1) * LANES]
    out[:, base : base + parts, :] = wide[...].reshape(k, parts, LANES).astype(BF16)


def exchange(
    owners,
    ranks,
    token_ref,
    forward_ref,
    backward_ref,
    got_raw,
    got_pair,
    got_meta,
    token,
    forward,
    backward,
    weights,
    wide,
    send_raw,
    send_pair,
    send_meta,
    sums,
    norm_send,
    norm_recv,
    raw_send,
    raw_recv,
    pair_send,
    pair_recv,
    meta_send,
    meta_recv,
    own_sem,
    load_sem,
    column_in,
):
    depth = owners // SIDE
    me = lax.axis_index("vocab")
    rank = lax.axis_index("state")
    z, y = me // SIDE, lax.rem(me, SIDE)
    parts = send_raw.shape[1]

    loads = [
        pltpu.make_async_copy(source, here, load_sem.at[i])
        for i, (source, here) in enumerate(
            ((token_ref, token), (forward_ref, forward), (backward_ref, backward))
        )
    ]
    for load in loads:
        load.start()

    ys = [lax.rem(y + dy, SIDE) for dy in range(SIDE)]

    barrier = pltpu.get_barrier_semaphore()

    def greet(**where):
        pl.semaphore_signal(barrier, inc=1, device_id=where, device_id_type=MESH)

    for dz in range(1, depth):
        greet(vocab=lax.rem(z + dz, depth) * SIDE + y)
    for dy in range(1, SIDE):
        greet(vocab=z * SIDE + ys[dy])
    for d in range(1, ranks):
        greet(state=lax.rem(rank + d, ranks))

    loads[0].wait()
    count, width = weights.shape
    owner, column, slot, first = route(token[...])
    owner_of = lax.broadcasted_iota(jnp.int32, (owners, count), 0).astype(F32)
    mine = owner_of == owner
    picks = [jnp.where(jnp.logical_and(mine, slot == s), 1.0, 0.0) for s in (0.0, 1.0, 2.0)]
    loads[1].wait()
    loads[2].wait()
    weights[...] = (forward[...].astype(F32) * backward[...].astype(F32)).astype(BF16)
    raw = jnp.dot(picks[0].astype(BF16), weights[...], preferred_element_type=F32)
    lay(raw, wide, send_raw, 0)

    def send(sources, there_z, dz, dy, there_y):
        there = there_z * SIDE + there_y
        for source, landing, sent, landed in sources:
            pltpu.make_async_remote_copy(
                src_ref=source.at[there],
                dst_ref=landing.at[dz * SIDE + dy],
                send_sem=sent,
                recv_sem=landed,
                device_id={"vocab": there},
                device_id_type=MESH,
            ).start()

    def push(sources, k, dys):
        dz = hop(k, z, depth)
        there_z = lax.rem(z + dz, depth)
        for dy in dys:
            send(sources, there_z, dz, dy, ys[dy])

    def push_all(sources, dys):
        def step(k, carry):
            push(sources, k, dys)
            return carry

        lax.fori_loop(0, depth - 1, step, 0)
        push(sources, depth - 1, [dy for dy in dys if dy])

    def push_column(sources):
        lead = depth // 4

        def reach(k, theres):
            there_z = column_order(k, depth)
            dz = lax.rem(there_z - z + depth, depth)
            for there_y in theres:
                dy = lax.rem(there_y - y + SIDE, SIDE)

                @pl.when(dz + dy != 0)
                def _(there_y=there_y, dy=dy):
                    send(sources, there_z, dz, dy, there_y)

        def begin(k, carry):
            reach(k, (0,))
            return carry

        def step(k, carry):
            reach(k + lead, (0,))
            reach(k, range(1, SIDE))
            return carry

        def finish(k, carry):
            reach(k, range(1, SIDE))
            return carry

        lax.fori_loop(0, lead, begin, 0)
        lax.fori_loop(0, depth - lead, step, 0)
        lax.fori_loop(depth - lead, depth, finish, 0)

    raw_ways = ((send_raw, got_raw, raw_send, raw_recv),)
    pair_ways = (
        (send_pair, got_pair, pair_send, pair_recv),
        (send_meta, got_meta, meta_send, meta_recv),
    )

    pl.semaphore_wait(barrier, depth - 1 + SIDE - 1 + ranks - 1)

    for dy in range(1, SIDE):
        pl.semaphore_signal(
            column_in, inc=1, device_id={"vocab": z * SIDE + ys[dy]}, device_id_type=MESH
        )
    push_all(raw_ways, [0])
    partial = lax.dot_general(
        jnp.ones((8, width), BF16), weights[...], (((1,), (1,)), ((), ())), preferred_element_type=F32
    )
    sums[rank] = partial[:1]
    for d in range(1, ranks):
        other = lax.rem(rank + d, ranks)
        pltpu.make_async_remote_copy(
            src_ref=sums.at[rank],
            dst_ref=sums.at[rank],
            send_sem=norm_send,
            recv_sem=norm_recv.at[d - 1],
            device_id={"state": other},
            device_id_type=MESH,
        ).start()
    pl.semaphore_wait(column_in, SIDE - 1)

    push_all(raw_ways, list(range(1, SIDE)))
    own_raw = pltpu.make_async_copy(send_raw.at[me], got_raw.at[0], own_sem.at[0])
    own_raw.start()

    for d in range(1, ranks):
        source = lax.rem(rank + ranks - d, ranks)
        pltpu.make_async_copy(sums.at[source], sums.at[source], norm_recv.at[d - 1]).wait()
    total = sums[0]
    for d in range(1, ranks):
        total = total + sums[d]
    scale = (ranks * width) / total
    eye = lax.broadcasted_iota(jnp.int32, (count, count), 0) == lax.broadcasted_iota(
        jnp.int32, (count, count), 1
    )
    scale_col = jnp.sum(jnp.where(eye, scale, 0.0), axis=1, keepdims=True)
    posterior = (weights[...].astype(F32) * scale_col).astype(BF16)
    for s in (1, 2):
        merged = jnp.dot(picks[s].astype(BF16), posterior, preferred_element_type=F32)
        lay(merged, wide, send_pair, (s - 1) * parts)
    lane = lax.broadcasted_iota(jnp.int32, (owners, LANES), 1)
    meta = jnp.zeros((owners, LANES), F32)
    for s in range(3):
        here = picks[s] * first
        ids = jnp.sum(here * (column + 1.0), axis=1, keepdims=True) - 1.0
        meta = jnp.where(lane == s, ids, meta)
    meta = jnp.where(lane == 3, jnp.sum(picks[0] * scale, axis=1, keepdims=True), meta)
    send_meta[...] = meta.reshape(owners, 1, LANES)

    push_column(pair_ways)
    own_pair = pltpu.make_async_copy(send_pair.at[me], got_pair.at[0], own_sem.at[1])
    own_pair.start()
    own_meta = pltpu.make_async_copy(send_meta.at[me], got_meta.at[0], own_sem.at[2])
    own_meta.start()

    own_raw.wait()
    own_pair.wait()
    own_meta.wait()
    rest = pl.ds(1, owners - 1)
    for ref, sem in ((got_raw, raw_recv), (got_pair, pair_recv), (got_meta, meta_recv)):
        pltpu.make_async_copy(ref.at[rest], ref.at[rest], sem).wait()
    for ref, sem in ((send_raw, raw_send), (send_pair, pair_send), (send_meta, meta_send)):
        pltpu.make_async_copy(ref.at[rest], ref.at[rest], sem).wait()
    others = pl.ds(1, ranks - 1)
    pltpu.make_async_copy(sums.at[others], sums.at[others], norm_send).wait()


def place(raw_ref, pair_ref, meta_ref, out_ref, wide_raw, wide_pair, onehot, block, sems):
    owners, parts, _ = raw_ref.shape
    odd, odd_pair = parts + 1, 2 * parts + 1
    for k in range(owners):
        wide_raw[k * odd : k * odd + parts, :] = raw_ref[k].astype(F32)
        wide_pair[k * odd_pair : k * odd_pair + 2 * parts, :] = pair_ref[k].astype(F32)
    meta = meta_ref[...].reshape(owners, LANES)
    ids = lax.broadcasted_iota(jnp.int32, (owners, V_DEV), 1).astype(F32)
    for s in range(3):
        hit = jnp.where(meta[:, s : s + 1] == ids, 1.0, 0.0)
        onehot[s * owners : (s + 1) * owners, :] = hit.astype(BF16)
    scale = meta[:, 3:4]
    copies = []
    for i in range(parts):
        lone = wide_raw[pl.ds(i, owners, stride=odd), :] * scale
        one = wide_pair[pl.ds(i, owners, stride=odd_pair), :]
        two = wide_pair[pl.ds(parts + i, owners, stride=odd_pair), :]
        rows = jnp.concatenate([lone.astype(BF16), one.astype(BF16), two.astype(BF16)], axis=0)
        counts = lax.dot_general(
            rows, onehot[...], (((0,), (0,)), ((), ())), preferred_element_type=F32
        )
        here = pl.ds(i * LANES, LANES)
        block[here, :] = counts.astype(BF16)
        copy = pltpu.make_async_copy(block.at[here], out_ref.at[here], sems.at[i])
        copy.start()
        copies.append(copy)
    for copy in copies:
        copy.wait()


def shards(token_ids, send_counts, forward_rows, backward_rows):
    owners = lax.axis_size("vocab")
    ranks = lax.axis_size("state")
    count, width = forward_rows.shape
    parts = width // LANES
    vmem = pl.BlockSpec(memory_space=pltpu.VMEM)
    anywhere = pl.BlockSpec(memory_space=pl.ANY)
    dma = pltpu.SemaphoreType.DMA
    got = pl.pallas_call(
        functools.partial(exchange, owners, ranks),
        out_shape=(
            jax.ShapeDtypeStruct((owners, parts, LANES), BF16),
            jax.ShapeDtypeStruct((owners, 2 * parts, LANES), BF16),
            jax.ShapeDtypeStruct((owners, 1, LANES), F32),
        ),
        in_specs=[pl.BlockSpec(memory_space=pltpu.HBM)] * 3,
        out_specs=(anywhere,) * 3,
        scratch_shapes=[
            pltpu.VMEM((1, count), jnp.int32),
            pltpu.VMEM((count, width), BF16),
            pltpu.VMEM((count, width), BF16),
            pltpu.VMEM((count, width), BF16),
            pltpu.VMEM((owners * parts, LANES), F32),
            pltpu.VMEM((owners, parts, LANES), BF16),
            pltpu.VMEM((owners, 2 * parts, LANES), BF16),
            pltpu.VMEM((owners, 1, LANES), F32),
            pltpu.VMEM((ranks, 1, count), F32),
            dma,
            dma((ranks - 1,)),
            dma,
            dma,
            dma,
            dma,
            dma,
            dma,
            dma((3,)),
            dma((3,)),
            pltpu.SemaphoreType.REGULAR,
        ],
        compiler_params=pltpu.CompilerParams(
            collective_id=0, has_side_effects=True, vmem_limit_bytes=32 * 1024 * 1024
        ),
    )(
        *(
            pltpu.with_memory_space_constraint(operand, pltpu.HBM)
            for operand in (token_ids.reshape(1, count), forward_rows, backward_rows)
        )
    )
    return pl.pallas_call(
        place,
        out_shape=jax.ShapeDtypeStruct((width, V_DEV), BF16),
        in_specs=[vmem] * 3,
        out_specs=anywhere,
        scratch_shapes=[
            pltpu.VMEM((owners * (parts + 1), LANES), F32),
            pltpu.VMEM((owners * (2 * parts + 1), LANES), F32),
            pltpu.VMEM((3 * owners, V_DEV), BF16),
            pltpu.VMEM((width, V_DEV), BF16),
            dma((parts,)),
        ],
        compiler_params=pltpu.CompilerParams(vmem_limit_bytes=32 * 1024 * 1024),
    )(*got)


def solution(mesh):
    placed = (P("vocab"), P("vocab"), P("vocab", "state"), P("vocab", "state"))
    return jax.shard_map(
        shards, mesh=mesh, in_specs=placed, out_specs=P("state", "vocab"), check_vma=False
    )
```

```python
import functools

import jax
import jax.numpy as jnp
from jax import lax
from jax.experimental import pallas as pl
from jax.experimental.pallas import tpu as pltpu
from jax.sharding import PartitionSpec as P

V_DEV = 1024
LANES = 128
SIDE = 4
MESH = pl.DeviceIdType.MESH
F32 = jnp.float32
BF16 = jnp.bfloat16


def hop(k, z, depth):
    half = depth // 2
    late = z // half
    last = k // (depth - 1)
    j = k // 2
    minus = lax.rem(k, 2)
    up = half - j
    down = half - 1 - j
    return lax.rem((1 - minus) * up + minus * (depth - down), depth)


def column_order(k, depth):
    return k // 2 + lax.rem(k, 2) * (depth // 2)


def route(token_row):
    n = token_row.shape[1]
    ids = token_row.astype(F32)
    up = lax.broadcasted_iota(jnp.int32, (n, n), 0)
    across = lax.broadcasted_iota(jnp.int32, (n, n), 1)
    eye = up == across
    before = up < across

    def turn(row):
        return jnp.sum(jnp.where(eye, row, 0.0), axis=1, keepdims=True)

    ids_col = turn(ids)
    owner = jnp.floor(ids * (1.0 / V_DEV))
    owner_col = jnp.floor(ids_col * (1.0 / V_DEV))
    same_id = jnp.where(ids_col == ids, 1.0, 0.0)
    same_owner = jnp.where(owner_col == owner, 1.0, 0.0)
    earlier = jnp.where(before, 1.0, 0.0)
    alone = jnp.where(jnp.sum(same_id, axis=0, keepdims=True) == 1.0, 1.0, 0.0)
    alone_before = jnp.sum(same_owner * earlier * turn(alone), axis=0, keepdims=True)
    raw = jnp.where(alone_before == 0.0, alone, 0.0)
    repeats = jnp.sum(same_id * earlier, axis=0, keepdims=True)
    leads = jnp.where(repeats == 0.0, 1.0 - raw, 0.0)
    lower = jnp.where(ids_col < ids, 1.0, 0.0)
    rank = jnp.sum(same_owner * lower * turn(leads), axis=0, keepdims=True)
    slot = jnp.where(raw == 1.0, 0.0, 1.0 + rank)
    first = jnp.where(repeats == 0.0, 1.0, 0.0)
    return owner, ids - owner * V_DEV, slot, first


def lay(rows, wide, out, base):
    k, width = rows.shape
    parts = width // LANES
    for i in range(parts):
        wide[pl.ds(i, k, stride=parts), :] = rows[:, i * LANES : (i + 1) * LANES]
    out[:, base : base + parts, :] = wide[: k * parts, :].reshape(k, parts, LANES).astype(BF16)


def exchange(
    owners,
    ranks,
    token_ref,
    forward_ref,
    backward_ref,
    got_raw,
    got_pair,
    got_meta,
    token,
    forward,
    backward,
    weights,
    wide,
    send_raw,
    send_pair,
    send_meta,
    sums,
    norm_send,
    norm_recv,
    raw_send,
    raw_recv,
    pair_send,
    pair_recv,
    meta_send,
    meta_recv,
    own_sem,
    load_sem,
    column_in,
):
    depth = owners // SIDE
    me = lax.axis_index("vocab")
    rank = lax.axis_index("state")
    z, y = me // SIDE, lax.rem(me, SIDE)
    parts = send_raw.shape[1]

    loads = [
        pltpu.make_async_copy(source, here, load_sem.at[i])
        for i, (source, here) in enumerate(
            ((token_ref, token), (forward_ref, forward), (backward_ref, backward))
        )
    ]
    for load in loads:
        load.start()

    ys = [lax.rem(y + dy, SIDE) for dy in range(SIDE)]

    barrier = pltpu.get_barrier_semaphore()

    def greet(**where):
        pl.semaphore_signal(barrier, inc=1, device_id=where, device_id_type=MESH)

    for dz in range(1, depth):
        greet(vocab=lax.rem(z + dz, depth) * SIDE + y)
    for dy in range(1, SIDE):
        greet(vocab=z * SIDE + ys[dy])
    for d in range(1, ranks):
        greet(state=lax.rem(rank + d, ranks))

    loads[0].wait()
    count, width = weights.shape
    owner, column, slot, first = route(token[...])
    owner_of = lax.broadcasted_iota(jnp.int32, (owners, count), 0).astype(F32)
    mine = owner_of == owner
    picks = [jnp.where(jnp.logical_and(mine, slot == s), 1.0, 0.0) for s in (0.0, 1.0, 2.0)]
    loads[1].wait()
    loads[2].wait()
    weights[...] = (forward[...].astype(F32) * backward[...].astype(F32)).astype(BF16)
    raw = jnp.dot(picks[0].astype(BF16), weights[...], preferred_element_type=F32)
    lay(raw, wide, send_raw, 0)

    def send(sources, there_z, dz, dy, there_y):
        there = there_z * SIDE + there_y
        for source, landing, sent, landed in sources:
            pltpu.make_async_remote_copy(
                src_ref=source.at[there],
                dst_ref=landing.at[dz * SIDE + dy],
                send_sem=sent,
                recv_sem=landed,
                device_id={"vocab": there},
                device_id_type=MESH,
            ).start()

    def push(sources, k, dys):
        dz = hop(k, z, depth)
        there_z = lax.rem(z + dz, depth)
        for dy in dys:
            send(sources, there_z, dz, dy, ys[dy])

    def push_all(sources, dys):
        def step(k, carry):
            push(sources, k, dys)
            return carry

        lax.fori_loop(0, depth - 1, step, 0)
        push(sources, depth - 1, [dy for dy in dys if dy])

    def push_column(sources):
        lead = depth // 4

        def reach(k, theres):
            there_z = column_order(k, depth)
            dz = lax.rem(there_z - z + depth, depth)
            for there_y in theres:
                dy = lax.rem(there_y - y + SIDE, SIDE)

                @pl.when(dz + dy != 0)
                def _(there_y=there_y, dy=dy):
                    send(sources, there_z, dz, dy, there_y)

        def begin(k, carry):
            reach(k, (0,))
            return carry

        def step(k, carry):
            reach(k + lead, (0,))
            reach(k, range(1, SIDE))
            return carry

        def finish(k, carry):
            reach(k, range(1, SIDE))
            return carry

        lax.fori_loop(0, lead, begin, 0)
        lax.fori_loop(0, depth - lead, step, 0)
        lax.fori_loop(depth - lead, depth, finish, 0)

    raw_ways = ((send_raw, got_raw, raw_send, raw_recv),)
    pair_ways = (
        (send_pair, got_pair, pair_send, pair_recv),
        (send_meta, got_meta, meta_send, meta_recv),
    )

    pl.semaphore_wait(barrier, depth - 1 + SIDE - 1 + ranks - 1)

    for dy in range(1, SIDE):
        pl.semaphore_signal(
            column_in, inc=1, device_id={"vocab": z * SIDE + ys[dy]}, device_id_type=MESH
        )
    push_all(raw_ways, [0])
    partial = lax.dot_general(
        jnp.ones((8, width), BF16), weights[...], (((1,), (1,)), ((), ())), preferred_element_type=F32
    )
    sums[rank] = partial[:1]
    for d in range(1, ranks):
        other = lax.rem(rank + d, ranks)
        pltpu.make_async_remote_copy(
            src_ref=sums.at[rank],
            dst_ref=sums.at[rank],
            send_sem=norm_send,
            recv_sem=norm_recv.at[d - 1],
            device_id={"state": other},
            device_id_type=MESH,
        ).start()
    pl.semaphore_wait(column_in, SIDE - 1)

    push_all(raw_ways, list(range(1, SIDE)))
    own_raw = pltpu.make_async_copy(send_raw.at[me], got_raw.at[0], own_sem.at[0])
    own_raw.start()

    for d in range(1, ranks):
        source = lax.rem(rank + ranks - d, ranks)
        pltpu.make_async_copy(sums.at[source], sums.at[source], norm_recv.at[d - 1]).wait()
    total = sums[0]
    for d in range(1, ranks):
        total = total + sums[d]
    scale = (ranks * width) / total
    eye = lax.broadcasted_iota(jnp.int32, (count, count), 0) == lax.broadcasted_iota(
        jnp.int32, (count, count), 1
    )
    scale_col = jnp.sum(jnp.where(eye, scale, 0.0), axis=1, keepdims=True)
    posterior = (weights[...].astype(F32) * scale_col).astype(BF16)
    for s in (1, 2):
        merged = jnp.dot(picks[s].astype(BF16), posterior, preferred_element_type=F32)
        lay(merged, wide, send_pair, (s - 1) * parts)
    lane = lax.broadcasted_iota(jnp.int32, (owners, LANES), 1)
    meta = jnp.zeros((owners, LANES), F32)
    for s in range(3):
        here = picks[s] * first
        ids = jnp.sum(here * (column + 1.0), axis=1, keepdims=True) - 1.0
        meta = jnp.where(lane == s, ids, meta)
    meta = jnp.where(lane == 3, jnp.sum(picks[0] * scale, axis=1, keepdims=True), meta)
    send_meta[...] = meta.reshape(owners, 1, LANES)

    push_column(pair_ways)
    own_pair = pltpu.make_async_copy(send_pair.at[me], got_pair.at[0], own_sem.at[1])
    own_pair.start()
    own_meta = pltpu.make_async_copy(send_meta.at[me], got_meta.at[0], own_sem.at[2])
    own_meta.start()

    own_raw.wait()
    own_pair.wait()
    own_meta.wait()
    rest = pl.ds(1, owners - 1)
    for ref, sem in ((got_raw, raw_recv), (got_pair, pair_recv), (got_meta, meta_recv)):
        pltpu.make_async_copy(ref.at[rest], ref.at[rest], sem).wait()
    for ref, sem in ((send_raw, raw_send), (send_pair, pair_send), (send_meta, meta_send)):
        pltpu.make_async_copy(ref.at[rest], ref.at[rest], sem).wait()
    others = pl.ds(1, ranks - 1)
    pltpu.make_async_copy(sums.at[others], sums.at[others], norm_send).wait()


def place(raw_ref, pair_ref, meta_ref, out_ref, wide_raw, wide_pair, onehot, block, sems):
    owners, parts, _ = raw_ref.shape
    odd, odd_pair = parts + 1, 2 * parts + 1
    for k in range(owners):
        wide_raw[k * odd : k * odd + parts, :] = raw_ref[k].astype(F32)
        wide_pair[k * odd_pair : k * odd_pair + 2 * parts, :] = pair_ref[k].astype(F32)
    meta = meta_ref[...].reshape(owners, LANES)
    ids = lax.broadcasted_iota(jnp.int32, (owners, V_DEV), 1).astype(F32)
    for s in range(3):
        hit = jnp.where(meta[:, s : s + 1] == ids, 1.0, 0.0)
        onehot[s * owners : (s + 1) * owners, :] = hit.astype(BF16)
    scale = meta[:, 3:4]
    copies = []
    for i in range(parts):
        lone = wide_raw[pl.ds(i, owners, stride=odd), :] * scale
        one = wide_pair[pl.ds(i, owners, stride=odd_pair), :]
        two = wide_pair[pl.ds(parts + i, owners, stride=odd_pair), :]
        rows = jnp.concatenate([lone.astype(BF16), one.astype(BF16), two.astype(BF16)], axis=0)
        counts = lax.dot_general(
            rows, onehot[...], (((0,), (0,)), ((), ())), preferred_element_type=F32
        )
        here = pl.ds(i * LANES, LANES)
        block[here, :] = counts.astype(BF16)
        copy = pltpu.make_async_copy(block.at[here], out_ref.at[here], sems.at[i])
        copy.start()
        copies.append(copy)
    for copy in copies:
        copy.wait()


def shards(token_ids, send_counts, forward_rows, backward_rows):
    owners = lax.axis_size("vocab")
    ranks = lax.axis_size("state")
    count, width = forward_rows.shape
    parts = width // LANES
    vmem = pl.BlockSpec(memory_space=pltpu.VMEM)
    anywhere = pl.BlockSpec(memory_space=pl.ANY)
    dma = pltpu.SemaphoreType.DMA
    got = pl.pallas_call(
        functools.partial(exchange, owners, ranks),
        out_shape=(
            jax.ShapeDtypeStruct((owners, parts, LANES), BF16),
            jax.ShapeDtypeStruct((owners, 2 * parts, LANES), BF16),
            jax.ShapeDtypeStruct((owners, 1, LANES), F32),
        ),
        in_specs=[pl.BlockSpec(memory_space=pltpu.HBM)] * 3,
        out_specs=(anywhere,) * 3,
        scratch_shapes=[
            pltpu.VMEM((1, count), jnp.int32),
            pltpu.VMEM((count, width), BF16),
            pltpu.VMEM((count, width), BF16),
            pltpu.VMEM((count, width), BF16),
            pltpu.VMEM(((owners + 1) * parts, LANES), F32),
            pltpu.VMEM((owners, parts, LANES), BF16),
            pltpu.VMEM((owners, 2 * parts, LANES), BF16),
            pltpu.VMEM((owners, 1, LANES), F32),
            pltpu.VMEM((ranks, 1, count), F32),
            dma,
            dma((ranks - 1,)),
            dma,
            dma,
            dma,
            dma,
            dma,
            dma,
            dma((3,)),
            dma((3,)),
            pltpu.SemaphoreType.REGULAR,
        ],
        compiler_params=pltpu.CompilerParams(
            collective_id=0, has_side_effects=True, vmem_limit_bytes=32 * 1024 * 1024
        ),
    )(
        *(
            pltpu.with_memory_space_constraint(operand, pltpu.HBM)
            for operand in (token_ids.reshape(1, count), forward_rows, backward_rows)
        )
    )
    return pl.pallas_call(
        place,
        out_shape=jax.ShapeDtypeStruct((width, V_DEV), BF16),
        in_specs=[vmem] * 3,
        out_specs=anywhere,
        scratch_shapes=[
            pltpu.VMEM(((owners + 1) * (parts + 1), LANES), F32),
            pltpu.VMEM(((owners + 1) * (2 * parts + 1), LANES), F32),
            pltpu.VMEM((3 * owners, V_DEV), BF16),
            pltpu.VMEM((width, V_DEV), BF16),
            dma((parts,)),
        ],
        compiler_params=pltpu.CompilerParams(vmem_limit_bytes=32 * 1024 * 1024),
    )(*got)


def solution(mesh):
    placed = (P("vocab"), P("vocab"), P("vocab", "state"), P("vocab", "state"))
    return jax.shard_map(
        shards, mesh=mesh, in_specs=placed, out_specs=P("state", "vocab"), check_vma=False
    )
```
